256 devices in a mesh: dp: 8 (over x, core), expert: 32 (over z, y).
Axes of the slice: x: 4, y: 4, z: 8, core: 2. Of those that a mesh axis runs over, the one named last changes fastest.
Arguments:
- tokens: bfloat16 [32768, 2048], P(('dp', 'expert')), may hold values from -6 to 6
- grad_out: bfloat16 [32768, 2048], P(('dp', 'expert')), may hold values from -6 to 6
- expert_ids: int32 [32768, 8], P(('dp', 'expert')), may hold values from 0 to 127, all different within a row; in each aligned block of 128 rows (0 to 127, 128 to 255, ...) at most 16 rows name the same one
- gate_probs: bfloat16 [32768, 8], P(('dp', 'expert')), may hold values from 0.019897461 to 0.5
- w_gate: bfloat16 [32, 2048, 768], P('expert'), may hold values from -0.125 to 0.125
- w_up: bfloat16 [32, 2048, 768], P('expert'), may hold values from -0.125 to 0.125
- w_down: bfloat16 [32, 768, 2048], P('expert'), may hold values from -0.21875 to 0.21875
Outputs:
- input_grad: bfloat16 [32768, 2048], P(('dp', 'expert'))
- gate_grad: float32 [32768, 8], P(('dp', 'expert'))
- gate_weight_grad: bfloat16 [32, 2048, 768], P('expert', 'dp')
- up_weight_grad: bfloat16 [32, 2048, 768], P('expert', 'dp')
- down_weight_grad: bfloat16 [32, 768, 2048], P('expert', None, 'dp')
The draws below stay inside these ranges and needn't reach their ends.
Inputs may be any that keep to these rules, and one draw needn't show every extreme that they name: `expert_ids`: each row names 8 different experts; among the rows of one device no expert is named more than 16 times, a bound that some block reaches.
All inputs are finite; a program needn't handle non-finite values.
Results may differ from the reference program's by a relative error of at most 0.019.
Values may be sent and summed in bfloat16 or wider, within the bound.
No kernel may reach another device: no remote copies, remote signals or barrier semaphores. Data moves between devices by JAX's collectives and lax.ppermute only.
A program may use at most 128 MiB of HBM per device.

```python
import math
import jax
import jax.numpy as jnp
import numpy as np
from jax import lax

D = 2048
HID = 768
EXPERTS = 128
TOPK = 8
TOK_DEV = 128
CAP = 16
LIVE = 32
TOKENS = 32768
N_DP = 8
N_EXPERT = 32


def shard_levels(stream_key, extent, shards, low, top_value):
    loudness, own = 1.0, jax.random.fold_in(stream_key, 6)
    for dim, blocks in shards:
        heights = jnp.exp(jax.random.uniform(jax.random.fold_in(own, dim), (blocks,), jnp.float32, low / len(shards), top_value / len(shards)))
        loudness = loudness * jnp.repeat(heights, extent[dim] // blocks).reshape([-1 if axis == dim else 1 for axis in range(len(extent))])
    return loudness


def shared_out(key, own, number, rows, amount, top, limit, lean):
    sequence = jax.random.permutation(key, amount)
    crowded, common = shares(amount, rows * top, limit, lean, True), shares(amount, rows * top, limit, lean, False)
    places = jnp.arange(amount)

    def named(tallies, turn):
        used = int((tallies > 0).sum())
        fixed = max(1, used // 4)
        moved = fixed + (places - fixed + turn * (used - fixed)) % max(1, amount - fixed)
        return jnp.zeros((amount,), jnp.int32).at[sequence[jnp.where(places < fixed, places, moved)]].set(jnp.asarray(tallies, jnp.int32))

    tallies = jnp.where(number % 4 == 0, named(crowded, number // 4), named(common, number - number // 4 - 1))
    mixed = jax.random.permutation(jax.random.fold_in(own, 3), amount)
    source_of, sink = mixed[0:amount // 2 * 2:2], mixed[1:amount // 2 * 2:2]
    margin = jnp.minimum(tallies[source_of] - 1, limit - tallies[sink]) // 2
    margin = jnp.where((source_of == sequence[0]) | (sink == sequence[0]) | (tallies[sink] == 0), 0, jnp.maximum(margin, 0))
    moved = jax.random.randint(jax.random.fold_in(own, 4), (amount // 2,), 0, 1 << 20) % (margin + 1)
    tallies = tallies.at[source_of].add(-moved).at[sink].add(moved)
    labels = jnp.searchsorted(jnp.cumsum(tallies), jnp.arange(rows * top), side="right").astype(jnp.int32)
    table = labels.reshape(top, rows).T
    table = table[jax.random.permutation(jax.random.fold_in(own, 1), rows)]
    turn = jax.random.randint(jax.random.fold_in(own, 2), (rows, 1), 0, top)
    return jnp.take_along_axis(table, (jnp.arange(top)[None, :] + turn) % top, axis=1)


def shares(number_of, total, reach, lean, full):
    loads = [(1 << 20) // math.isqrt(rank ** lean) + 1 for rank in range(1, number_of + 1)]
    largest = reach if full else min(reach, max(-(-total // number_of), total * loads[0] // sum(loads)))
    least = 1 if total - largest >= number_of - 1 else 0
    holding, surplus = [largest] + [least] * (number_of - 1), total - largest - least * (number_of - 1)
    while surplus > 0:
        movable = [i for i in range(1, number_of) if holding[i] < largest] or [i for i in range(1, number_of) if holding[i] < reach]
        whole, left = sum([loads[i] for i in movable]), surplus
        for i in movable:
            more = min(reach - holding[i], max(1, left * loads[i] // whole), surplus)
            holding[i] = holding[i] + more
            surplus = surplus - more
    return np.array(holding)


def noise(own_key, extent, spread, reach, cuts=(), held_as=jnp.bfloat16):
    factor_of = shard_levels(own_key, extent, cuts, -0.22, 0.18) if cuts else 1.0
    values = jax.random.normal(own_key, extent, jnp.float32) * spread * factor_of
    return jnp.minimum(jnp.maximum(values, -reach), reach).astype(held_as)


def setup_inputs(seed: int = 0) -> dict:
    key_list = jax.random.split(jax.random.key(seed), 8)
    tokens = noise(key_list[0], (TOKENS, D), 1.0, 6.0, ((0, 256),))
    grad_out = noise(key_list[1], (TOKENS, D), 1.0, 6.0, ((0, 256),))
    expert_ids_keys = jax.random.split(jax.random.fold_in(key_list[2], 1), TOKENS // TOK_DEV)
    expert_ids_turns = jax.random.permutation(jax.random.fold_in(key_list[2], 3), TOKENS // TOK_DEV)
    expert_ids = jax.vmap(lambda own, number: shared_out(jax.random.fold_in(key_list[2], 2), own, number, TOK_DEV, EXPERTS, TOPK, CAP, 2))(expert_ids_keys, expert_ids_turns).reshape((TOKENS, TOPK))
    gate_probs = jnp.clip(jnp.exp(math.log(0.5) - 3.224016 * jax.random.uniform(key_list[3], (TOKENS, TOPK), jnp.float32) ** shard_levels(key_list[3], (TOKENS, TOPK), ((0, 256),), -0.2, 0.2)), 0.019897461, 0.5).astype(jnp.bfloat16)
    w_gate = noise(key_list[4], (LIVE, D, HID), D ** -0.5, 0.125, ((0, 32),))
    w_up = noise(key_list[5], (LIVE, D, HID), D ** -0.5, 0.125, ((0, 32),))
    w_down = noise(key_list[6], (LIVE, HID, D), HID ** -0.5, 0.21875, ((0, 32),))
    return {"tokens": tokens, "grad_out": grad_out, "expert_ids": expert_ids, "gate_probs": gate_probs, "w_gate": w_gate, "w_up": w_up, "w_down": w_down}


def slot_math(x_rows, dy_rows, g_rows, w_gate, w_up, w_down):
    gate_pre = jnp.dot(x_rows, w_gate, preferred_element_type=jnp.float32)
    up_pre = jnp.dot(x_rows, w_up, preferred_element_type=jnp.float32)
    sig = jax.nn.sigmoid(gate_pre)
    act = gate_pre * sig
    hidden = (act * up_pre).astype(jnp.bfloat16)
    gvals = g_rows.astype(jnp.float32)[:, None]
    scaled_dy = (gvals * dy_rows.astype(jnp.float32)).astype(jnp.bfloat16)
    back = lax.dot_general(dy_rows, w_down, (((1,), (1,)), ((), ())), preferred_element_type=jnp.float32)
    router = jnp.sum(back * hidden.astype(jnp.float32), axis=1)
    dhidden = gvals * back
    d_up = (dhidden * act).astype(jnp.bfloat16)
    d_gatepre = (dhidden * up_pre * (sig * (1.0 + gate_pre * (1.0 - sig)))).astype(jnp.bfloat16)
    dx_rows = lax.dot_general(d_gatepre, w_gate, (((1,), (1,)), ((), ())), preferred_element_type=jnp.float32)
    dx_rows = dx_rows + lax.dot_general(d_up, w_up, (((1,), (1,)), ((), ())), preferred_element_type=jnp.float32)
    return scaled_dy, hidden, d_gatepre, d_up, dx_rows, router


def reference(tokens, grad_out, expert_ids, gate_probs, w_gate, w_up, w_down):
    ndev = N_DP * N_EXPERT
    count = TOK_DEV * TOPK
    ids = expert_ids.reshape(ndev, count)
    hits = (ids[:, :, None] == jnp.arange(N_EXPERT, dtype=jnp.int32)[None, None, :]).astype(jnp.int32)
    rank = jnp.sum((jnp.cumsum(hits, axis=1) - hits) * hits, axis=2).astype(jnp.int32)
    slot = jnp.where(ids < N_EXPERT, ids * CAP + rank, N_EXPERT * CAP).astype(jnp.int32)
    table = jnp.full((ndev, N_EXPERT * CAP + 1), -1, jnp.int32)
    rowsel = jnp.arange(ndev, dtype=jnp.int32)[:, None] * jnp.ones((1, count), jnp.int32)
    table = table.at[rowsel, slot].set(jnp.arange(count, dtype=jnp.int32)[None, :] * jnp.ones((ndev, 1), jnp.int32))
    table = table[:, :N_EXPERT * CAP].reshape(ndev, N_EXPERT, CAP).transpose(1, 0, 2)
    gate_flat = gate_probs.reshape(-1)

    def one_expert(carry, inputs):
        dx_total, dg_total = carry
        local, wg, wu, wd = inputs
        valid = (local >= 0).reshape(-1)
        gidx = jnp.where(local >= 0, jnp.arange(ndev, dtype=jnp.int32)[:, None] * count + local, 0).reshape(-1).astype(jnp.int32)
        tok = (gidx // TOPK).astype(jnp.int32)
        x_rows = jnp.where(valid[:, None], tokens[tok], jnp.zeros((), jnp.bfloat16))
        dy_rows = jnp.where(valid[:, None], grad_out[tok], jnp.zeros((), jnp.bfloat16))
        g_rows = jnp.where(valid, gate_flat[gidx], jnp.zeros((), jnp.bfloat16))
        scaled_dy, hidden, d_gatepre, d_up, dx_rows, router = slot_math(x_rows, dy_rows, g_rows, wg, wu, wd)
        rows = N_EXPERT * CAP
        xs = x_rows.reshape(N_DP, rows, -1).astype(jnp.float32)
        ys = scaled_dy.reshape(N_DP, rows, -1).astype(jnp.float32)
        hs = hidden.reshape(N_DP, rows, -1).astype(jnp.float32)
        gs = d_gatepre.reshape(N_DP, rows, -1).astype(jnp.float32)
        us = d_up.reshape(N_DP, rows, -1).astype(jnp.float32)
        part_g = jnp.einsum("srd,srh->sdh", xs, gs).astype(jnp.bfloat16).astype(jnp.float32)
        part_u = jnp.einsum("srd,srh->sdh", xs, us).astype(jnp.bfloat16).astype(jnp.float32)
        part_d = jnp.einsum("srh,srd->shd", hs, ys).astype(jnp.bfloat16).astype(jnp.float32)
        grad_g = jnp.sum(part_g, axis=0).astype(jnp.bfloat16)
        grad_u = jnp.sum(part_u, axis=0).astype(jnp.bfloat16)
        grad_d = jnp.sum(part_d, axis=0).astype(jnp.bfloat16)
        dump = jnp.where(valid, tok, TOKENS).astype(jnp.int32)
        dx_total = dx_total.at[dump].add(dx_rows)
        dump_a = jnp.where(valid, gidx, TOKENS * TOPK).astype(jnp.int32)
        dg_total = dg_total.at[dump_a].add(router)
        return (dx_total, dg_total), (grad_g, grad_u, grad_d)

    init = (jnp.zeros((TOKENS + 1, D), jnp.float32), jnp.zeros((TOKENS * TOPK + 1,), jnp.float32))
    (dx_total, dg_total), grads = lax.scan(one_expert, init, (table, w_gate, w_up, w_down))
    input_grad = dx_total[:TOKENS].astype(jnp.bfloat16)
    gate_grad = dg_total[:TOKENS * TOPK].reshape(TOKENS, TOPK)
    return input_grad, gate_grad, grads[0], grads[1], grads[2]
```

```python
import functools
import jax
import jax.numpy as jnp
from jax import lax
from jax.experimental import pallas as pl
from jax.experimental.pallas import tpu as pltpu
from jax.sharding import PartitionSpec as P

CAP = 16
LANES = 128
BF = jnp.bfloat16
F32 = jnp.float32
VMEM_LIMIT = 56 * 1024 * 1024


def mm(a, b):
    return jnp.dot(a, b, preferred_element_type=F32)


def mm_nt(a, b):
    return lax.dot_general(a, b, (((1,), (1,)), ((), ())), preferred_element_type=F32)


def params(vmem=VMEM_LIMIT):
    return pltpu.CompilerParams(vmem_limit_bytes=vmem)


def cost(flops, nbytes):
    return pl.CostEstimate(flops=flops, bytes_accessed=nbytes, transcendentals=0)


def route_kernel(groups, ids_ref, probs_ref, tok_ref, dy_ref, out_ref, s_ref, sg_ref):
    topk, tok_dev = ids_ref.shape

    @pl.when(pl.program_id(0) == 0)
    def _():
        ids = ids_ref[...]
        probs = probs_ref[...].astype(F32)
        expert = lax.broadcasted_iota(jnp.int32, (groups, tok_dev), 0)
        hits = jnp.zeros((groups, tok_dev), F32)
        gate = jnp.zeros((groups, tok_dev), F32)
        for k in range(topk):
            hit = ids[k : k + 1] == expert
            hits = jnp.where(hit, 1.0, hits)
            gate = jnp.where(hit, probs[k : k + 1], gate)
        row = lax.broadcasted_iota(jnp.int32, (tok_dev, tok_dev), 0)
        col = lax.broadcasted_iota(jnp.int32, (tok_dev, tok_dev), 1)
        before = jnp.where(row < col, 1.0, 0.0).astype(BF)
        rank = mm(hits.astype(BF), before)
        rank = jnp.where(hits > 0.0, rank, -1.0).astype(jnp.int32)
        slot = lax.broadcasted_iota(jnp.int32, (groups, CAP, tok_dev), 1)
        sel = rank[:, None, :] == slot
        s_ref[...] = jnp.where(sel, 1.0, 0.0).reshape(groups * CAP, tok_dev).astype(BF)
        sg_ref[...] = (
            jnp.where(sel, jnp.broadcast_to(gate[:, None, :], sel.shape), 0.0)
            .reshape(groups * CAP, tok_dev)
            .astype(BF)
        )

    cols = tok_ref.shape[1]
    x = mm(s_ref[...], tok_ref[...]).astype(BF)
    out_ref[:, :CAP, :] = x.reshape(groups, CAP, cols)
    gy = mm(sg_ref[...], dy_ref[...]).astype(BF)
    out_ref[:, CAP:, :] = gy.reshape(groups, CAP, cols)


def route(ids, probs, tokens, grad_out, groups):
    tok_dev, width = tokens.shape
    topk = ids.shape[0]
    slots = groups * CAP
    steps = 4
    cols = width // steps
    const = lambda j: (0, 0)
    return pl.pallas_call(
        functools.partial(route_kernel, groups),
        grid=(steps,),
        in_specs=[
            pl.BlockSpec((topk, tok_dev), const),
            pl.BlockSpec((topk, tok_dev), const),
            pl.BlockSpec((tok_dev, cols), lambda j: (0, j)),
            pl.BlockSpec((tok_dev, cols), lambda j: (0, j)),
        ],
        out_specs=[
            pl.BlockSpec((groups, 2 * CAP, cols), lambda j: (0, 0, j)),
            pl.BlockSpec((slots, tok_dev), const),
        ],
        out_shape=[
            jax.ShapeDtypeStruct((groups, 2 * CAP, width), BF),
            jax.ShapeDtypeStruct((slots, tok_dev), BF),
        ],
        scratch_shapes=[pltpu.VMEM((slots, tok_dev), BF)],
        compiler_params=params(),
        cost_estimate=cost(4 * slots * tok_dev * width, 4 * (slots + tok_dev) * width),
        name="route",
    )(ids, probs, tokens, grad_out)


def mm_tn(a, b):
    return lax.dot_general(a, b, (((0,), (0,)), ((), ())), preferred_element_type=F32)


def expert_kernel(
    recv_hbm, wg_hbm, wu_hbm, wd_hbm, dx_hbm, dw_hbm, x_s, gy_s, wg_s, wu_s, wd_s, dx_s, dw_s, in_sems, out_sems
):
    groups, _, width = recv_hbm.shape
    rows = groups * CAP
    parts = dw_hbm.shape[0]
    loads = [
        pltpu.make_async_copy(recv_hbm.at[:, :CAP, :], x_s, in_sems.at[0]),
        pltpu.make_async_copy(wg_hbm, wg_s, in_sems.at[1]),
        pltpu.make_async_copy(wu_hbm, wu_s, in_sems.at[2]),
        pltpu.make_async_copy(recv_hbm.at[:, CAP:, :], gy_s, in_sems.at[3]),
        pltpu.make_async_copy(wd_hbm, wd_s, in_sems.at[4]),
    ]
    for c in loads:
        c.start()
    stores = []

    def store(src, dst):
        c = pltpu.make_async_copy(src, dst, out_sems.at[len(stores)])
        c.start()
        stores.append(c)

    def weight_part(w, rows_v, units):
        dw_s[w] = mm_tn(rows_v, units).astype(BF).reshape(dw_s.shape[1:])
        store(dw_s.at[w], dw_hbm.at[:, w])

    loads[0].wait()
    loads[1].wait()
    x = x_s[...].reshape(rows, width)
    a = mm(x, wg_s[...])
    loads[2].wait()
    u = mm(x, wu_s[...])
    s = jax.nn.sigmoid(a)
    act = a * s
    fa = u * (s * (1.0 + a * (1.0 - s)))
    h = (act * u).astype(BF)
    loads[3].wait()
    gy = gy_s[...].reshape(rows, width)
    weight_part(0, gy, h)
    loads[4].wait()
    dh = mm_nt(gy, wd_s[...])
    da = (dh * fa).astype(BF)
    du = (dh * act).astype(BF)
    r = jnp.sum(dh * h.astype(F32), axis=1, keepdims=True)
    dx_s[:, width:] = jnp.broadcast_to(r, (rows, LANES)).astype(BF)
    weight_part(1, x, da)
    weight_part(2, x, du)
    cut = width // 2
    for lo, hi, end in ((0, cut, cut), (cut, width, width + LANES)):
        dx = mm_nt(da, wg_s[lo:hi, :]) + mm_nt(du, wu_s[lo:hi, :])
        dx_s[:, lo:hi] = dx.astype(BF)
        store(dx_s.at[:, lo:end], dx_hbm.at[:, lo:end])
    for c in stores:
        c.wait()


def expert_pass(recv, wg, wu, wd, parts):
    groups, _, width = recv.shape
    rows = groups * CAP
    hid = wg.shape[1]
    part = width // parts
    hbm = pl.BlockSpec(memory_space=pl.ANY)
    return pl.pallas_call(
        expert_kernel,
        in_specs=[hbm] * 4,
        out_specs=[hbm] * 2,
        out_shape=[
            jax.ShapeDtypeStruct((rows, width + LANES), BF),
            jax.ShapeDtypeStruct((parts, 3, part, hid), BF),
        ],
        scratch_shapes=[
            pltpu.VMEM((groups, CAP, width), BF),
            pltpu.VMEM((groups, CAP, width), BF),
            pltpu.VMEM(wg.shape, BF),
            pltpu.VMEM(wu.shape, BF),
            pltpu.VMEM(wd.shape, BF),
            pltpu.VMEM((rows, width + LANES), BF),
            pltpu.VMEM((3, parts, part, hid), BF),
            pltpu.SemaphoreType.DMA((5,)),
            pltpu.SemaphoreType.DMA((5,)),
        ],
        compiler_params=params(),
        cost_estimate=cost(16 * rows * width * hid, 2 * (3 * rows * width + 6 * width * hid)),
        name="expert_pass",
    )(recv, wg, wu, wd)


def unpack_kernel(sum_ref, g_ref, u_ref, d_ref):
    d_ref[0] = sum_ref[0, 0].T
    g_ref[0] = sum_ref[0, 1]
    u_ref[0] = sum_ref[0, 2]


def unpack(total):
    _, _, part, hid = total.shape
    return pl.pallas_call(
        unpack_kernel,
        out_shape=[
            jax.ShapeDtypeStruct((1, part, hid), BF),
            jax.ShapeDtypeStruct((1, part, hid), BF),
            jax.ShapeDtypeStruct((1, hid, part), BF),
        ],
        compiler_params=params(),
        name="unpack",
    )(total)


def combine_kernel(width, s_ref, ids_ref, probs_ref, back_ref, dx_ref, gg_ref):
    groups = s_ref.shape[0] // CAP
    topk, tok_dev = ids_ref.shape
    s = s_ref[...]
    dx_ref[...] = mm(s.T, back_ref[:, :width]).astype(BF)
    r = back_ref[:, width:].astype(F32) * s.astype(F32)
    r = jnp.sum(r.reshape(groups, CAP, tok_dev), axis=1)
    ids = ids_ref[...]
    expert = lax.broadcasted_iota(jnp.int32, (groups, tok_dev), 0)
    for k in range(topk):
        v = jnp.sum(jnp.where(expert == ids[k : k + 1], r, 0.0), axis=0, keepdims=True)
        gg_ref[k : k + 1] = v / probs_ref[k : k + 1].astype(F32)


def combine(s, ids, probs, back):
    slots, tok_dev = s.shape
    width = back.shape[1] - LANES
    return pl.pallas_call(
        functools.partial(combine_kernel, width),
        out_shape=[
            jax.ShapeDtypeStruct((tok_dev, width), BF),
            jax.ShapeDtypeStruct(ids.shape, F32),
        ],
        compiler_params=params(),
        cost_estimate=cost(2 * slots * tok_dev * width, 2 * (slots + tok_dev) * width),
        name="combine",
    )(s, ids, probs, back)


def exchange(rows):
    return lax.all_to_all(rows, "expert", split_axis=0, concat_axis=0, tiled=True)


def on_device(tokens, grad_out, expert_ids, gate_probs, w_gate, w_up, w_down):
    groups = lax.axis_size("expert")
    parts = lax.axis_size("dp")
    ids, probs = expert_ids.T, gate_probs.T
    send, sel = route(ids, probs, tokens, grad_out, groups)
    recv = exchange(send)
    dx, dw = expert_pass(recv, w_gate[0], w_up[0], w_down[0], parts)
    slots = dx.shape[0]
    total = lax.psum_scatter(dw, "dp", scatter_dimension=0, tiled=True)
    back = exchange(dx.reshape(groups, CAP, -1)).reshape(slots, -1)
    input_grad, gate_grad = combine(sel, ids, probs, back)
    return input_grad, gate_grad.T, *unpack(total)


def solution(mesh):
    row = P(("dp", "expert"), None)
    per_expert = P("expert", None, None)
    return jax.shard_map(
        on_device,
        mesh=mesh,
        in_specs=(row, row, row, row, per_expert, per_expert, per_expert),
        out_specs=(row, row, P("expert", "dp", None), P("expert", "dp", None), P("expert", None, "dp")),
        check_vma=False,
    )
```

```python
import functools
import jax
import jax.numpy as jnp
from jax import lax
from jax.experimental import pallas as pl
from jax.experimental.pallas import tpu as pltpu
from jax.sharding import PartitionSpec as P

CAP = 16
LANES = 128
BF = jnp.bfloat16
F32 = jnp.float32
VMEM_LIMIT = 56 * 1024 * 1024


def mm(a, b):
    return jnp.dot(a, b, preferred_element_type=F32)


def mm_nt(a, b):
    return lax.dot_general(a, b, (((1,), (1,)), ((), ())), preferred_element_type=F32)


def params(vmem=VMEM_LIMIT):
    return pltpu.CompilerParams(vmem_limit_bytes=vmem)


def cost(flops, nbytes):
    return pl.CostEstimate(flops=flops, bytes_accessed=nbytes, transcendentals=0)


def route_kernel(groups, ids_ref, probs_ref, tok_ref, dy_ref, out_ref, s_ref, sg_ref):
    topk, tok_dev = ids_ref.shape

    @pl.when(pl.program_id(0) == 0)
    def _():
        ids = ids_ref[...]
        probs = probs_ref[...].astype(F32)
        expert = lax.broadcasted_iota(jnp.int32, (groups, tok_dev), 0)
        hits = jnp.zeros((groups, tok_dev), F32)
        gate = jnp.zeros((groups, tok_dev), F32)
        for k in range(topk):
            hit = ids[k : k + 1] == expert
            hits = jnp.where(hit, 1.0, hits)
            gate = jnp.where(hit, probs[k : k + 1], gate)
        row = lax.broadcasted_iota(jnp.int32, (tok_dev, tok_dev), 0)
        col = lax.broadcasted_iota(jnp.int32, (tok_dev, tok_dev), 1)
        before = jnp.where(row < col, 1.0, 0.0).astype(BF)
        rank = mm(hits.astype(BF), before)
        rank = jnp.where(hits > 0.0, rank, -1.0).astype(jnp.int32)
        slot = lax.broadcasted_iota(jnp.int32, (groups, CAP, tok_dev), 1)
        sel = rank[:, None, :] == slot
        s_ref[...] = jnp.where(sel, 1.0, 0.0).reshape(groups * CAP, tok_dev).astype(BF)
        sg_ref[...] = (
            jnp.where(sel, jnp.broadcast_to(gate[:, None, :], sel.shape), 0.0)
            .reshape(groups * CAP, tok_dev)
            .astype(BF)
        )

    cols = tok_ref.shape[1]
    x = mm(s_ref[...], tok_ref[...]).astype(BF)
    out_ref[:, :CAP, :] = x.reshape(groups, CAP, cols)
    gy = mm(sg_ref[...], dy_ref[...]).astype(BF)
    out_ref[:, CAP:, :] = gy.reshape(groups, CAP, cols)


def route(ids, probs, tokens, grad_out, groups):
    tok_dev, width = tokens.shape
    topk = ids.shape[0]
    slots = groups * CAP
    steps = 4
    cols = width // steps
    const = lambda j: (0, 0)
    return pl.pallas_call(
        functools.partial(route_kernel, groups),
        grid=(steps,),
        in_specs=[
            pl.BlockSpec((topk, tok_dev), const),
            pl.BlockSpec((topk, tok_dev), const),
            pl.BlockSpec((tok_dev, cols), lambda j: (0, j)),
            pl.BlockSpec((tok_dev, cols), lambda j: (0, j)),
        ],
        out_specs=[
            pl.BlockSpec((groups, 2 * CAP, cols), lambda j: (0, 0, j)),
            pl.BlockSpec((slots, tok_dev), const),
        ],
        out_shape=[
            jax.ShapeDtypeStruct((groups, 2 * CAP, width), BF),
            jax.ShapeDtypeStruct((slots, tok_dev), BF),
        ],
        scratch_shapes=[pltpu.VMEM((slots, tok_dev), BF)],
        compiler_params=params(),
        cost_estimate=cost(4 * slots * tok_dev * width, 4 * (slots + tok_dev) * width),
        name="route",
    )(ids, probs, tokens, grad_out)


def mm_tn(a, b):
    return lax.dot_general(a, b, (((0,), (0,)), ((), ())), preferred_element_type=F32)


def put_parts(tmp_ref, down, gate, up):
    part, hid = gate.shape[0] // 2, gate.shape[1]
    half = hid // 2
    for c in range(2):
        cols = slice(c * part, (c + 1) * part)
        for i in range(2):
            tmp_ref[c, i, 2] = down[i * half : (i + 1) * half, cols]
        for lo in range(0, hid, LANES):
            b, q = lo // part, lo % part
            rows = slice(c * part + q, c * part + q + LANES)
            for w, t in ((0, gate), (1, up)):
                tmp_ref[c, lo // half, w, lo % half : lo % half + LANES] = t[rows, b * part : (b + 1) * part]


def expert_kernel(
    place_ref, recv_hbm, wg_hbm, wu_hbm, wd_hbm, dx_hbm, own_hbm, other_hbm,
    x_s, gy_s, wg_s, wu_s, wd_s, dx_s, tmp_s, in_sems, dx_sems, own_sems, other_sems,
):
    groups, _, width = recv_hbm.shape
    rows = groups * CAP
    loads = [
        pltpu.make_async_copy(recv_hbm.at[:, :CAP, :], x_s, in_sems.at[0]),
        pltpu.make_async_copy(wg_hbm, wg_s, in_sems.at[1]),
        pltpu.make_async_copy(wu_hbm, wu_s, in_sems.at[2]),
        pltpu.make_async_copy(recv_hbm.at[:, CAP:, :], gy_s, in_sems.at[3]),
        pltpu.make_async_copy(wd_hbm, wd_s, in_sems.at[4]),
    ]
    for c in loads:
        c.start()
    stores = []

    def store(src, dst, sem):
        c = pltpu.make_async_copy(src, dst, sem)
        c.start()
        stores.append(c)

    loads[0].wait()
    loads[1].wait()
    x = x_s[...].reshape(rows, width)
    a = mm(x, wg_s[...])
    loads[2].wait()
    u = mm(x, wu_s[...])
    s = jax.nn.sigmoid(a)
    act = a * s
    fa = u * (s * (1.0 + a * (1.0 - s)))
    h = (act * u).astype(BF)
    loads[3].wait()
    loads[4].wait()
    dh = mm_nt(gy_s[...].reshape(rows, width), wd_s[...])
    da = (dh * fa).astype(BF)
    du = (dh * act).astype(BF)
    r = jnp.sum(dh * h.astype(F32), axis=1, keepdims=True)
    dx_s[:, width:] = jnp.broadcast_to(r, (rows, LANES)).astype(BF)
    core, pair = place_ref[0], width // 4
    for j in range(4):
        cols = pl.ds(pl.multiple_of(place_ref[1 + j] * pair, pair), pair)
        xc = x_s[:, :, cols].reshape(rows, pair)
        gyc = gy_s[:, :, cols].reshape(rows, pair)
        put_parts(tmp_s.at[j], mm_tn(h, gyc).astype(BF), mm_tn(xc, da).astype(BF), mm_tn(xc, du).astype(BF))
        store(tmp_s.at[j, core], own_hbm.at[j], own_sems.at[j])
        store(tmp_s.at[j, 1 - core], other_hbm.at[j], other_sems.at[j])
    cut = width // 2
    for i, lo, hi, end in ((0, 0, cut, cut), (1, cut, width, width + LANES)):
        dx = mm_nt(da, wg_s[lo:hi, :]) + mm_nt(du, wu_s[lo:hi, :])
        dx_s[:, lo:hi] = dx.astype(BF)
        store(dx_s.at[:, lo:end], dx_hbm.at[:, lo:end], dx_sems.at[i])
    for c in stores:
        c.wait()


def expert_pass(place, recv, wg, wu, wd):
    groups, _, width = recv.shape
    rows = groups * CAP
    hid = wg.shape[1]
    part = width // 8
    hbm = pl.BlockSpec(memory_space=pl.ANY)
    parts = jax.ShapeDtypeStruct((4, 2, 3, hid // 2, part), BF)
    return pl.pallas_call(
        expert_kernel,
        in_specs=[pl.BlockSpec(memory_space=pltpu.SMEM)] + [hbm] * 4,
        out_specs=[hbm] * 3,
        out_shape=[jax.ShapeDtypeStruct((rows, width + LANES), BF), parts, parts],
        scratch_shapes=[
            pltpu.VMEM((groups, CAP, width), BF),
            pltpu.VMEM((groups, CAP, width), BF),
            pltpu.VMEM(wg.shape, BF),
            pltpu.VMEM(wu.shape, BF),
            pltpu.VMEM(wd.shape, BF),
            pltpu.VMEM((rows, width + LANES), BF),
            pltpu.VMEM((4, 2, 2, 3, hid // 2, part), BF),
            pltpu.SemaphoreType.DMA((5,)),
            pltpu.SemaphoreType.DMA((2,)),
            pltpu.SemaphoreType.DMA((4,)),
            pltpu.SemaphoreType.DMA((4,)),
        ],
        compiler_params=params(),
        cost_estimate=cost(16 * rows * width * hid, 2 * (3 * rows * width + 6 * width * hid)),
        name="expert_pass",
    )(place, recv, wg, wu, wd)


def reduce_parts(own, other):
    swap = lambda t: lax.ppermute(t, "dp", [(i, i ^ 1) for i in range(8)])
    shift = lambda t, d: lax.ppermute(t, "dp", [(i, (i + 2 * d) % 8) for i in range(8)])
    add = lambda *t: sum(v.astype(F32) for v in t).astype(BF)
    other = swap(other)
    from_left = shift(add(own[0, 0], other[0, 0]), 1)
    from_right = shift(add(own[0, 1], other[0, 1]), -1)
    plain_left = shift(add(own[1, 1], other[1, 1]), 1)
    plain_right = shift(add(own[2, 0], other[2, 0]), -1)
    sum_left = shift(add(own[1, 0], other[1, 0], from_left), 1)
    sum_right = shift(add(own[2, 1], other[2, 1], from_right), -1)
    return own, other, plain_left, plain_right, sum_left, sum_right


def finish_kernel(own_ref, other_ref, pl_ref, pr_ref, sl_ref, sr_ref, g_ref, u_ref, d_ref):
    part = g_ref.shape[1]
    half = own_ref.shape[3]
    low = own_ref[0, 0].astype(F32) + other_ref[0, 0].astype(F32)
    low = (low + pr_ref[...].astype(F32) + sl_ref[...].astype(F32)).astype(BF)
    high = own_ref[0, 1].astype(F32) + other_ref[0, 1].astype(F32)
    high = (high + pl_ref[...].astype(F32) + sr_ref[...].astype(F32)).astype(BF)
    d_ref[0, :half] = low[2]
    d_ref[0, half:] = high[2]
    for w, ref in ((0, g_ref), (1, u_ref)):
        for b in range(2 * half // part):
            for lo in range(b * part, (b + 1) * part, LANES):
                src = low[w, lo : lo + LANES] if lo < half else high[w, lo - half : lo - half + LANES]
                ref[0, lo - b * part : lo - b * part + LANES, b * part : (b + 1) * part] = src


def finish(own, other, *recvd):
    _, _, _, half, part = own.shape
    hid = 2 * half
    mine = pl.BlockSpec((1, 2, 3, half, part), lambda i: (3, 0, 0, 0, 0))
    whole = pl.BlockSpec((3, half, part), lambda i: (0, 0, 0))
    zero = lambda i: (0, 0, 0)
    return pl.pallas_call(
        finish_kernel,
        grid=(1,),
        in_specs=[mine, mine] + [whole] * 4,
        out_specs=[
            pl.BlockSpec((1, part, hid), zero),
            pl.BlockSpec((1, part, hid), zero),
            pl.BlockSpec((1, hid, part), zero),
        ],
        out_shape=[
            jax.ShapeDtypeStruct((1, part, hid), BF),
            jax.ShapeDtypeStruct((1, part, hid), BF),
            jax.ShapeDtypeStruct((1, hid, part), BF),
        ],
        compiler_params=params(),
        name="finish",
    )(own, other, *recvd)


def combine_kernel(width, s_ref, ids_ref, probs_ref, back_ref, dx_ref, gg_ref):
    groups = s_ref.shape[0] // CAP
    topk, tok_dev = ids_ref.shape
    s = s_ref[...]
    dx_ref[...] = mm(s.T, back_ref[:, :width]).astype(BF)
    r = back_ref[:, width:].astype(F32) * s.astype(F32)
    r = jnp.sum(r.reshape(groups, CAP, tok_dev), axis=1)
    ids = ids_ref[...]
    expert = lax.broadcasted_iota(jnp.int32, (groups, tok_dev), 0)
    for k in range(topk):
        v = jnp.sum(jnp.where(expert == ids[k : k + 1], r, 0.0), axis=0, keepdims=True)
        gg_ref[k : k + 1] = v / probs_ref[k : k + 1].astype(F32)


def combine(s, ids, probs, back):
    slots, tok_dev = s.shape
    width = back.shape[1] - LANES
    return pl.pallas_call(
        functools.partial(combine_kernel, width),
        out_shape=[
            jax.ShapeDtypeStruct((tok_dev, width), BF),
            jax.ShapeDtypeStruct(ids.shape, F32),
        ],
        compiler_params=params(),
        cost_estimate=cost(2 * slots * tok_dev * width, 2 * (slots + tok_dev) * width),
        name="combine",
    )(s, ids, probs, back)


def exchange(rows):
    return lax.all_to_all(rows, "expert", split_axis=0, concat_axis=0, tiled=True)


def on_device(tokens, grad_out, expert_ids, gate_probs, w_gate, w_up, w_down):
    groups = lax.axis_size("expert")
    ids, probs = expert_ids.T, gate_probs.T
    send, sel = route(ids, probs, tokens, grad_out, groups)
    recv = exchange(send)
    p = lax.axis_index("dp")
    x, core = p // 2, p % 2
    place = jnp.stack([core, (x + 2) % 4, (x + 1) % 4, (x + 3) % 4, x])
    dx, own, other = expert_pass(place, recv, w_gate[0], w_up[0], w_down[0])
    slots = dx.shape[0]
    back = exchange(dx.reshape(groups, CAP, -1)).reshape(slots, -1)
    grads = finish(*reduce_parts(own, other))
    sel, *grads = lax.optimization_barrier((sel, *grads))
    input_grad, gate_grad = combine(sel, ids, probs, back)
    return input_grad, gate_grad.T, *grads


def solution(mesh):
    row = P(("dp", "expert"), None)
    per_expert = P("expert", None, None)
    return jax.shard_map(
        on_device,
        mesh=mesh,
        in_specs=(row, row, row, row, per_expert, per_expert, per_expert),
        out_specs=(row, row, P("expert", "dp", None), P("expert", "dp", None), P("expert", None, "dp")),
        check_vma=False,
    )
```

```python
import functools
import jax
import jax.numpy as jnp
from jax import lax
from jax.experimental import pallas as pl
from jax.experimental.pallas import tpu as pltpu
from jax.sharding import PartitionSpec as P

CAP = 16
LANES = 128
BF = jnp.bfloat16
F32 = jnp.float32
VMEM_LIMIT = 56 * 1024 * 1024
SMALL = 16 * 1024 * 1024


def mm(a, b):
    return jnp.dot(a, b, preferred_element_type=F32)


def mm_nt(a, b):
    return lax.dot_general(a, b, (((1,), (1,)), ((), ())), preferred_element_type=F32)


def params(vmem=VMEM_LIMIT):
    return pltpu.CompilerParams(vmem_limit_bytes=vmem)


def cost(flops, nbytes):
    return pl.CostEstimate(flops=flops, bytes_accessed=nbytes, transcendentals=0)


def route_kernel(groups, ids_ref, probs_ref, tok_ref, dy_ref, out_ref, s_ref, sg_ref):
    topk, tok_dev = ids_ref.shape

    @pl.when(pl.program_id(0) == 0)
    def _():
        ids = ids_ref[...]
        probs = probs_ref[...].astype(F32)
        expert = lax.broadcasted_iota(jnp.int32, (groups, tok_dev), 0)
        hits = jnp.zeros((groups, tok_dev), F32)
        gate = jnp.zeros((groups, tok_dev), F32)
        for k in range(topk):
            hit = ids[k : k + 1] == expert
            hits = jnp.where(hit, 1.0, hits)
            gate = jnp.where(hit, probs[k : k + 1], gate)
        row = lax.broadcasted_iota(jnp.int32, (tok_dev, tok_dev), 0)
        col = lax.broadcasted_iota(jnp.int32, (tok_dev, tok_dev), 1)
        before = jnp.where(row < col, 1.0, 0.0).astype(BF)
        rank = mm(hits.astype(BF), before)
        rank = jnp.where(hits > 0.0, rank, -1.0).astype(jnp.int32)
        slot = lax.broadcasted_iota(jnp.int32, (groups, CAP, tok_dev), 1)
        sel = rank[:, None, :] == slot
        s_ref[...] = jnp.where(sel, 1.0, 0.0).reshape(groups * CAP, tok_dev).astype(BF)
        sg_ref[...] = (
            jnp.where(sel, jnp.broadcast_to(gate[:, None, :], sel.shape), 0.0)
            .reshape(groups * CAP, tok_dev)
            .astype(BF)
        )

    cols = tok_ref.shape[1]
    x = mm(s_ref[...], tok_ref[...]).astype(BF)
    out_ref[:, :CAP, :] = x.reshape(groups, CAP, cols)
    gy = mm(sg_ref[...], dy_ref[...]).astype(BF)
    out_ref[:, CAP:, :] = gy.reshape(groups, CAP, cols)


def route(ids, probs, tokens, grad_out, groups):
    tok_dev, width = tokens.shape
    topk = ids.shape[0]
    slots = groups * CAP
    steps = 4
    cols = width // steps
    const = lambda j: (0, 0)
    return pl.pallas_call(
        functools.partial(route_kernel, groups),
        grid=(steps,),
        in_specs=[
            pl.BlockSpec((topk, tok_dev), const),
            pl.BlockSpec((topk, tok_dev), const),
            pl.BlockSpec((tok_dev, cols), lambda j: (0, j)),
            pl.BlockSpec((tok_dev, cols), lambda j: (0, j)),
        ],
        out_specs=[
            pl.BlockSpec((groups, 2 * CAP, cols), lambda j: (0, 0, j)),
            pl.BlockSpec((slots, tok_dev), const),
        ],
        out_shape=[
            jax.ShapeDtypeStruct((groups, 2 * CAP, width), BF),
            jax.ShapeDtypeStruct((slots, tok_dev), BF),
        ],
        scratch_shapes=[pltpu.VMEM((slots, tok_dev), BF)],
        compiler_params=params(),
        cost_estimate=cost(4 * slots * tok_dev * width, 4 * (slots + tok_dev) * width),
        name="route",
    )(ids, probs, tokens, grad_out)


def mm_tn(a, b):
    return lax.dot_general(a, b, (((0,), (0,)), ((), ())), preferred_element_type=F32)


def put_parts(tmp_ref, down, gate, up):
    part, hid = gate.shape[0] // 2, gate.shape[1]
    half = hid // 2
    for c in range(2):
        cols = slice(c * part, (c + 1) * part)
        for i in range(2):
            tmp_ref[c, i, 2] = down[i * half : (i + 1) * half, cols]
        for lo in range(0, hid, LANES):
            b, q = lo // part, lo % part
            rows = slice(c * part + q, c * part + q + LANES)
            for w, t in ((0, gate), (1, up)):
                tmp_ref[c, lo // half, w, lo % half : lo % half + LANES] = t[rows, b * part : (b + 1) * part]


def expert_kernel(
    place_ref, recv_hbm, wg_hbm, wu_hbm, wd_hbm, dx_hbm, own_hbm, other_hbm,
    x_s, gy_s, wg_s, wu_s, wd_s, dx_s, tmp_s, in_sems, dx_sems, own_sems, other_sems,
):
    groups, _, width = recv_hbm.shape
    rows = groups * CAP
    loads = [
        pltpu.make_async_copy(recv_hbm.at[:, :CAP, :], x_s, in_sems.at[0]),
        pltpu.make_async_copy(wg_hbm, wg_s, in_sems.at[1]),
        pltpu.make_async_copy(wu_hbm, wu_s, in_sems.at[2]),
        pltpu.make_async_copy(recv_hbm.at[:, CAP:, :], gy_s, in_sems.at[3]),
        pltpu.make_async_copy(wd_hbm, wd_s, in_sems.at[4]),
    ]
    for c in loads:
        c.start()
    stores = []

    def store(src, dst, sem):
        c = pltpu.make_async_copy(src, dst, sem)
        c.start()
        stores.append(c)

    loads[0].wait()
    loads[1].wait()
    x = x_s[...].reshape(rows, width)
    a = mm(x, wg_s[...])
    loads[2].wait()
    u = mm(x, wu_s[...])
    s = jax.nn.sigmoid(a)
    act = a * s
    fa = u * (s * (1.0 + a * (1.0 - s)))
    h = (act * u).astype(BF)
    loads[3].wait()
    loads[4].wait()
    dh = mm_nt(gy_s[...].reshape(rows, width), wd_s[...])
    da = (dh * fa).astype(BF)
    du = (dh * act).astype(BF)
    r = jnp.sum(dh * h.astype(F32), axis=1, keepdims=True)
    dx_s[:, width:] = jnp.broadcast_to(r, (rows, LANES)).astype(BF)
    core, pair = place_ref[0], width // 4
    for j in range(4):
        cols = pl.ds(pl.multiple_of(place_ref[1 + j] * pair, pair), pair)
        xc = x_s[:, :, cols].reshape(rows, pair)
        gyc = gy_s[:, :, cols].reshape(rows, pair)
        put_parts(tmp_s.at[j], mm_tn(h, gyc).astype(BF), mm_tn(xc, da).astype(BF), mm_tn(xc, du).astype(BF))
        store(tmp_s.at[j, core], own_hbm.at[j], own_sems.at[j])
        store(tmp_s.at[j, 1 - core], other_hbm.at[j], other_sems.at[j])
    cut = width // 2
    for i, lo, hi, end in ((0, 0, cut, cut), (1, cut, width, width + LANES)):
        dx = mm_nt(da, wg_s[lo:hi, :]) + mm_nt(du, wu_s[lo:hi, :])
        dx_s[:, lo:hi] = dx.astype(BF)
        store(dx_s.at[:, lo:end], dx_hbm.at[:, lo:end], dx_sems.at[i])
    for c in stores:
        c.wait()


def expert_pass(place, recv, wg, wu, wd):
    groups, _, width = recv.shape
    rows = groups * CAP
    hid = wg.shape[1]
    part = width // 8
    hbm = pl.BlockSpec(memory_space=pl.ANY)
    parts = jax.ShapeDtypeStruct((4, 2, 3, hid // 2, part), BF)
    return pl.pallas_call(
        expert_kernel,
        in_specs=[pl.BlockSpec(memory_space=pltpu.SMEM)] + [hbm] * 4,
        out_specs=[hbm] * 3,
        out_shape=[jax.ShapeDtypeStruct((rows, width + LANES), BF), parts, parts],
        scratch_shapes=[
            pltpu.VMEM((groups, CAP, width), BF),
            pltpu.VMEM((groups, CAP, width), BF),
            pltpu.VMEM(wg.shape, BF),
            pltpu.VMEM(wu.shape, BF),
            pltpu.VMEM(wd.shape, BF),
            pltpu.VMEM((rows, width + LANES), BF),
            pltpu.VMEM((4, 2, 2, 3, hid // 2, part), BF),
            pltpu.SemaphoreType.DMA((5,)),
            pltpu.SemaphoreType.DMA((2,)),
            pltpu.SemaphoreType.DMA((4,)),
            pltpu.SemaphoreType.DMA((4,)),
        ],
        compiler_params=params(),
        cost_estimate=cost(16 * rows * width * hid, 2 * (3 * rows * width + 6 * width * hid)),
        name="expert_pass",
    )(place, recv, wg, wu, wd)


def reduce_parts(own, other):
    swap = lambda t: lax.ppermute(t, "dp", [(i, i ^ 1) for i in range(8)])
    shift = lambda t, d: lax.ppermute(t, "dp", [(i, (i + 2 * d) % 8) for i in range(8)])
    add = lambda *t: sum(v.astype(F32) for v in t).astype(BF)
    other = swap(other)
    from_left = shift(add(own[0, 0], other[0, 0]), 1)
    from_right = shift(add(own[0, 1], other[0, 1]), -1)
    plain_left = shift(add(own[1, 1], other[1, 1]), 1)
    plain_right = shift(add(own[2, 0], other[2, 0]), -1)
    sum_left = shift(add(own[1, 0], other[1, 0], from_left), 1)
    sum_right = shift(add(own[2, 1], other[2, 1], from_right), -1)
    return partial(own, other, plain_left, plain_right), sum_left, sum_right


def partial_kernel(own_ref, other_ref, left_ref, right_ref, out_ref):
    for i, ref in ((0, right_ref), (1, left_ref)):
        t = own_ref[0, i].astype(F32) + other_ref[0, i].astype(F32) + ref[...].astype(F32)
        out_ref[i] = t.astype(BF)


def partial(own, other, left, right):
    _, _, _, half, part = own.shape
    mine = pl.BlockSpec((1, 2, 3, half, part), lambda i: (3, 0, 0, 0, 0))
    whole = pl.BlockSpec((3, half, part), lambda i: (0, 0, 0))
    return pl.pallas_call(
        partial_kernel,
        grid=(1,),
        in_specs=[mine, mine, whole, whole],
        out_specs=pl.BlockSpec((2, 3, half, part), lambda i: (0, 0, 0, 0)),
        out_shape=jax.ShapeDtypeStruct((2, 3, half, part), BF),
        compiler_params=params(SMALL),
        name="partial",
    )(own, other, left, right)


def finish_kernel(sum_ref, left_ref, right_ref, g_ref, u_ref, d_ref):
    part = g_ref.shape[1]
    half = sum_ref.shape[2]
    low = (sum_ref[0].astype(F32) + left_ref[...].astype(F32)).astype(BF)
    high = (sum_ref[1].astype(F32) + right_ref[...].astype(F32)).astype(BF)
    d_ref[0, :half] = low[2]
    d_ref[0, half:] = high[2]
    for w, ref in ((0, g_ref), (1, u_ref)):
        for lo in range(0, 2 * half, LANES):
            b, q = lo // part, lo % part
            src = low[w, lo : lo + LANES] if lo < half else high[w, lo - half : lo - half + LANES]
            ref[0, q : q + LANES, b * part : (b + 1) * part] = src


def finish(total, left, right):
    _, _, half, part = total.shape
    hid = 2 * half
    return pl.pallas_call(
        finish_kernel,
        out_shape=[
            jax.ShapeDtypeStruct((1, part, hid), BF),
            jax.ShapeDtypeStruct((1, part, hid), BF),
            jax.ShapeDtypeStruct((1, hid, part), BF),
        ],
        compiler_params=params(SMALL),
        name="finish",
    )(total, left, right)


def combine_kernel(s_ref, ids_ref, probs_ref, back_ref, r_ref, dx_ref, gg_ref, st_ref):
    groups = s_ref.shape[0] // CAP
    topk, tok_dev = ids_ref.shape

    @pl.when(pl.program_id(0) == 0)
    def _():
        s = s_ref[...]
        st_ref[...] = s.T
        r = r_ref[...].astype(F32) * s.astype(F32)
        r = jnp.sum(r.reshape(groups, CAP, tok_dev), axis=1)
        ids = ids_ref[...]
        expert = lax.broadcasted_iota(jnp.int32, (groups, tok_dev), 0)
        for k in range(topk):
            v = jnp.sum(jnp.where(expert == ids[k : k + 1], r, 0.0), axis=0, keepdims=True)
            gg_ref[k : k + 1] = v / probs_ref[k : k + 1].astype(F32)

    dx_ref[...] = mm(st_ref[...], back_ref[...]).astype(BF)


def combine(s, ids, probs, back):
    slots, tok_dev = s.shape
    width = back.shape[1] - LANES
    steps = 2
    cols = width // steps
    const = lambda j: (0, 0)
    return pl.pallas_call(
        combine_kernel,
        grid=(steps,),
        in_specs=[
            pl.BlockSpec(s.shape, const),
            pl.BlockSpec(ids.shape, const),
            pl.BlockSpec(ids.shape, const),
            pl.BlockSpec((slots, cols), lambda j: (0, j)),
            pl.BlockSpec((slots, LANES), lambda j: (0, width // LANES)),
        ],
        out_specs=[pl.BlockSpec((tok_dev, cols), lambda j: (0, j)), pl.BlockSpec(ids.shape, const)],
        out_shape=[
            jax.ShapeDtypeStruct((tok_dev, width), BF),
            jax.ShapeDtypeStruct(ids.shape, F32),
        ],
        scratch_shapes=[pltpu.VMEM((tok_dev, slots), BF)],
        compiler_params=params(SMALL),
        cost_estimate=cost(2 * slots * tok_dev * width, 2 * (slots + tok_dev) * width),
        name="combine",
    )(s, ids, probs, back, back)


def exchange(rows):
    return lax.all_to_all(rows, "expert", split_axis=0, concat_axis=0, tiled=True)


def exchange(rows):
    return lax.all_to_all(rows, "expert", split_axis=0, concat_axis=0, tiled=True)


def on_device(tokens, grad_out, expert_ids, gate_probs, w_gate, w_up, w_down):
    groups = lax.axis_size("expert")
    ids, probs = expert_ids.T, gate_probs.T
    send, sel = route(ids, probs, tokens, grad_out, groups)
    recv = exchange(send)
    p = lax.axis_index("dp")
    x, core = p // 2, p % 2
    place = jnp.stack([core, (x + 2) % 4, (x + 1) % 4, (x + 3) % 4, x])
    dx, own, other = expert_pass(place, recv, w_gate[0], w_up[0], w_down[0])
    slots = dx.shape[0]
    back = exchange(dx.reshape(groups, CAP, -1)).reshape(slots, -1)
    grads = finish(*reduce_parts(own, other))
    sel, *grads = lax.optimization_barrier((sel, *grads))
    input_grad, gate_grad = combine(sel, ids, probs, back)
    return input_grad, gate_grad.T, *grads


def solution(mesh):
    row = P(("dp", "expert"), None)
    per_expert = P("expert", None, None)
    return jax.shard_map(
        on_device,
        mesh=mesh,
        in_specs=(row, row, row, row, per_expert, per_expert, per_expert),
        out_specs=(row, row, P("expert", "dp", None), P("expert", "dp", None), P("expert", None, "dp")),
        check_vma=False,
    )
```

```python
import functools
import jax
import jax.numpy as jnp
from jax import lax
from jax.experimental import pallas as pl
from jax.experimental.pallas import tpu as pltpu
from jax.sharding import PartitionSpec as P

CAP = 16
LANES = 128
BF = jnp.bfloat16
F32 = jnp.float32
VMEM_LIMIT = 56 * 1024 * 1024
SMALL = 16 * 1024 * 1024


def mm(a, b):
    return jnp.dot(a, b, preferred_element_type=F32)


def mm_nt(a, b):
    return lax.dot_general(a, b, (((1,), (1,)), ((), ())), preferred_element_type=F32)


def params(vmem=VMEM_LIMIT):
    return pltpu.CompilerParams(vmem_limit_bytes=vmem)


def cost(flops, nbytes):
    return pl.CostEstimate(flops=flops, bytes_accessed=nbytes, transcendentals=0)


def route_kernel(groups, ids_ref, probs_ref, tok_ref, dy_ref, out_ref, s_ref, sg_ref):
    topk, tok_dev = ids_ref.shape

    @pl.when(pl.program_id(0) == 0)
    def _():
        ids = ids_ref[...]
        probs = probs_ref[...].astype(F32)
        expert = lax.broadcasted_iota(jnp.int32, (groups, tok_dev), 0)
        hits = jnp.zeros((groups, tok_dev), F32)
        gate = jnp.zeros((groups, tok_dev), F32)
        for k in range(topk):
            hit = ids[k : k + 1] == expert
            hits = jnp.where(hit, 1.0, hits)
            gate = jnp.where(hit, probs[k : k + 1], gate)
        row = lax.broadcasted_iota(jnp.int32, (tok_dev, tok_dev), 0)
        col = lax.broadcasted_iota(jnp.int32, (tok_dev, tok_dev), 1)
        before = jnp.where(row < col, 1.0, 0.0).astype(BF)
        rank = mm(hits.astype(BF), before)
        rank = jnp.where(hits > 0.0, rank, -1.0).astype(jnp.int32)
        slot = lax.broadcasted_iota(jnp.int32, (groups, CAP, tok_dev), 1)
        sel = rank[:, None, :] == slot
        s_ref[...] = jnp.where(sel, 1.0, 0.0).reshape(groups * CAP, tok_dev).astype(BF)
        sg_ref[...] = (
            jnp.where(sel, jnp.broadcast_to(gate[:, None, :], sel.shape), 0.0)
            .reshape(groups * CAP, tok_dev)
            .astype(BF)
        )

    cols = tok_ref.shape[1]
    x = mm(s_ref[...], tok_ref[...]).astype(BF)
    out_ref[:, :CAP, :] = x.reshape(groups, CAP, cols)
    gy = mm(sg_ref[...], dy_ref[...]).astype(BF)
    out_ref[:, CAP:, :] = gy.reshape(groups, CAP, cols)


def route(ids, probs, tokens, grad_out, groups):
    tok_dev, width = tokens.shape
    topk = ids.shape[0]
    slots = groups * CAP
    steps = 2
    cols = width // steps
    const = lambda j: (0, 0)
    return pl.pallas_call(
        functools.partial(route_kernel, groups),
        grid=(steps,),
        in_specs=[
            pl.BlockSpec((topk, tok_dev), const),
            pl.BlockSpec((topk, tok_dev), const),
            pl.BlockSpec((tok_dev, cols), lambda j: (0, j)),
            pl.BlockSpec((tok_dev, cols), lambda j: (0, j)),
        ],
        out_specs=[
            pl.BlockSpec((groups, 2 * CAP, cols), lambda j: (0, 0, j)),
            pl.BlockSpec((slots, tok_dev), const),
        ],
        out_shape=[
            jax.ShapeDtypeStruct((groups, 2 * CAP, width), BF),
            jax.ShapeDtypeStruct((slots, tok_dev), BF),
        ],
        scratch_shapes=[pltpu.VMEM((slots, tok_dev), BF)],
        compiler_params=params(),
        cost_estimate=cost(4 * slots * tok_dev * width, 4 * (slots + tok_dev) * width),
        name="route",
    )(ids, probs, tokens, grad_out)


def mm_tn(a, b):
    return lax.dot_general(a, b, (((0,), (0,)), ((), ())), preferred_element_type=F32)


def rows_kernel(
    place_ref, recv_hbm, wg_hbm, wu_hbm, wd_hbm, dx_hbm, own_hbm, send_hbm,
    x_s, gy_s, wg_s, wu_s, wd_s, dx_s, units_s, in_sems, out_sems, cols_sems,
):
    groups, _, width = recv_hbm.shape
    rows = groups * CAP
    loads = [
        pltpu.make_async_copy(recv_hbm.at[:, :CAP, :], x_s, in_sems.at[0]),
        pltpu.make_async_copy(wg_hbm, wg_s, in_sems.at[1]),
        pltpu.make_async_copy(wu_hbm, wu_s, in_sems.at[2]),
        pltpu.make_async_copy(recv_hbm.at[:, CAP:, :], gy_s, in_sems.at[3]),
        pltpu.make_async_copy(wd_hbm, wd_s, in_sems.at[4]),
    ]
    for c in loads:
        c.start()
    stores = []

    def store(src, dst, sem):
        c = pltpu.make_async_copy(src, dst, sem)
        c.start()
        stores.append(c)

    loads[0].wait()
    loads[1].wait()
    x = x_s[...].reshape(rows, width)
    a = mm(x, wg_s[...])
    loads[2].wait()
    u = mm(x, wu_s[...])
    s = jax.nn.sigmoid(a)
    act = a * s
    fa = u * (s * (1.0 + a * (1.0 - s)))
    units_s[0] = (act * u).astype(BF).reshape(units_s.shape[1:])
    loads[3].wait()
    loads[4].wait()
    core, part = place_ref[0], width // 8
    for i, dst in ((0, own_hbm), (1, send_hbm)):
        for k in range(9):
            which = 2 * place_ref[1 + k // 2 % 4] + (core if i == 0 else 1 - core)
            cols = pl.ds(pl.multiple_of(which * part, part), part)
            src = gy_s if k % 2 else x_s
            at = slice(k % 3 * part, (k % 3 + 1) * part)
            store(src.at[:, :, cols], dst.at[3 + k // 3, :, :, at], cols_sems.at[9 * i + k])
    dh = mm_nt(gy_s[...].reshape(rows, width), wd_s[...])
    units_s[1] = (dh * fa).astype(BF).reshape(units_s.shape[1:])
    units_s[2] = (dh * act).astype(BF).reshape(units_s.shape[1:])
    store(units_s, own_hbm.at[:3], out_sems.at[2])
    store(units_s, send_hbm.at[:3], out_sems.at[3])
    h, da, du = (units_s[i].reshape(rows, units_s.shape[3]) for i in range(3))
    r = jnp.sum(dh * h.astype(F32), axis=1, keepdims=True)
    dx_s[:, width:] = jnp.broadcast_to(r, (rows, LANES)).astype(BF)
    cut = width // 2
    for i, lo, hi, end in ((0, 0, cut, cut), (1, cut, width, width + LANES)):
        dx = mm_nt(da, wg_s[lo:hi, :]) + mm_nt(du, wu_s[lo:hi, :])
        dx_s[:, lo:hi] = dx.astype(BF)
        store(dx_s.at[:, lo:end], dx_hbm.at[:, lo:end], out_sems.at[i])
    for c in stores:
        c.wait()


def rows_pass(place, recv, wg, wu, wd):
    groups, _, width = recv.shape
    rows = groups * CAP
    hid = wg.shape[1]
    hbm = pl.BlockSpec(memory_space=pl.ANY)
    pack = jax.ShapeDtypeStruct((6, groups, CAP, hid), BF)
    return pl.pallas_call(
        rows_kernel,
        in_specs=[pl.BlockSpec(memory_space=pltpu.SMEM)] + [hbm] * 4,
        out_specs=[hbm] * 3,
        out_shape=[jax.ShapeDtypeStruct((rows, width + LANES), BF), pack, pack],
        scratch_shapes=[
            pltpu.VMEM((groups, CAP, width), BF),
            pltpu.VMEM((groups, CAP, width), BF),
            pltpu.VMEM(wg.shape, BF),
            pltpu.VMEM(wu.shape, BF),
            pltpu.VMEM(wd.shape, BF),
            pltpu.VMEM((rows, width + LANES), BF),
            pltpu.VMEM((3, groups, CAP, hid), BF),
            pltpu.SemaphoreType.DMA((5,)),
            pltpu.SemaphoreType.DMA((4,)),
            pltpu.SemaphoreType.DMA((18,)),
        ],
        compiler_params=params(),
        cost_estimate=cost(10 * rows * width * hid, 2 * (3 * rows * width + 3 * width * hid)),
        name="rows_pass",
    )(place, recv, wg, wu, wd)


def grad(refs, chunk, w, lo, hi):
    k = 2 * chunk + (1 if w == 0 else 0)
    total = 0.0
    for ref in refs:
        _, groups, cap, hid = ref.shape
        part = hid // 3
        cols = ref[3 + k // 3, :, :, k % 3 * part : (k % 3 + 1) * part].reshape(groups * cap, part)
        total = total + mm_tn(cols, ref[w, :, :, lo:hi].reshape(groups * cap, hi - lo))
    return total


def first_kernel(*refs):
    refs, (far_a, far_b, near_b, near_a) = refs[:2], refs[2:]
    hid = refs[0].shape[3]
    half = hid // 2
    for w in range(3):
        t = grad(refs, 0, w, 0, hid).astype(BF)
        far_a[w] = t[:, :half]
        far_b[w] = t[:, half:]
        near_b[w] = grad(refs, 1, w, half, hid).astype(BF)
        near_a[w] = grad(refs, 2, w, 0, half).astype(BF)


def second_kernel(*refs):
    refs, (left, right, sum_left, sum_right) = refs[:2], refs[2:]
    hid = refs[0].shape[3]
    half = hid // 2
    for w in range(3):
        sum_left[w] = (grad(refs, 1, w, 0, half) + left[w].astype(F32)).astype(BF)
        sum_right[w] = (grad(refs, 2, w, half, hid) + right[w].astype(F32)).astype(BF)


def third_kernel(*refs):
    refs, (left, right, out) = refs[:2], refs[2:]
    hid = refs[0].shape[3]
    half = hid // 2
    for w in range(3):
        t = grad(refs, 3, w, 0, hid)
        out[0, w] = (t[:, :half] + right[w].astype(F32)).astype(BF)
        out[1, w] = (t[:, half:] + left[w].astype(F32)).astype(BF)


def part_call(kernel, name, outs, *args):
    return pl.pallas_call(
        kernel,
        out_shape=outs,
        compiler_params=params(20 * 1024 * 1024),
        name=name,
    )(*args)


def reduce_parts(own, send):
    swap = lambda t: lax.ppermute(t, "dp", [(i, i ^ 1) for i in range(8)])
    shift = lambda t, d: lax.ppermute(t, "dp", [(i, (i + 2 * d) % 8) for i in range(8)])
    rows = own, swap(send)
    hid = own.shape[3]
    part, half = hid // 3, hid // 2
    piece = jax.ShapeDtypeStruct((3, part, half), BF)
    far_a, far_b, near_b, near_a = part_call(first_kernel, "first_parts", [piece] * 4, *rows)
    from_left, from_right = shift(far_a, 1), shift(far_b, -1)
    plain_left, plain_right = shift(near_b, 1), shift(near_a, -1)
    sums = part_call(second_kernel, "second_parts", [piece] * 2, *rows, from_left, from_right)
    mine = jax.ShapeDtypeStruct((2, 3, part, half), BF)
    total = part_call(third_kernel, "third_parts", mine, *rows, plain_left, plain_right)
    return total, shift(sums[0], 1), shift(sums[1], -1)


def finish_kernel(sum_ref, left_ref, right_ref, g_ref, u_ref, d_ref):
    half = sum_ref.shape[3]
    for i, ref in ((0, left_ref), (1, right_ref)):
        t = (sum_ref[i].astype(F32) + ref[...].astype(F32)).astype(BF)
        cols = slice(i * half, (i + 1) * half)
        d_ref[0, cols, :] = t[0].T
        g_ref[0, :, cols] = t[1]
        u_ref[0, :, cols] = t[2]


def finish(total, left, right):
    _, _, part, half = total.shape
    hid = 2 * half
    return pl.pallas_call(
        finish_kernel,
        out_shape=[
            jax.ShapeDtypeStruct((1, part, hid), BF),
            jax.ShapeDtypeStruct((1, part, hid), BF),
            jax.ShapeDtypeStruct((1, hid, part), BF),
        ],
        compiler_params=params(SMALL),
        name="finish",
    )(total, left, right)


def combine_kernel(s_ref, ids_ref, probs_ref, back_ref, r_ref, dx_ref, gg_ref, st_ref):
    groups = s_ref.shape[0] // CAP
    topk, tok_dev = ids_ref.shape

    @pl.when(pl.program_id(0) == 0)
    def _():
        s = s_ref[...]
        st_ref[...] = s.T
        r = r_ref[...].astype(F32) * s.astype(F32)
        r = jnp.sum(r.reshape(groups, CAP, tok_dev), axis=1)
        ids = ids_ref[...]
        expert = lax.broadcasted_iota(jnp.int32, (groups, tok_dev), 0)
        for k in range(topk):
            v = jnp.sum(jnp.where(expert == ids[k : k + 1], r, 0.0), axis=0, keepdims=True)
            gg_ref[k : k + 1] = v / probs_ref[k : k + 1].astype(F32)

    dx_ref[...] = mm(st_ref[...], back_ref[...]).astype(BF)


def combine(s, ids, probs, back):
    slots, tok_dev = s.shape
    width = back.shape[1] - LANES
    steps = 1
    cols = width // steps
    const = lambda j: (0, 0)
    return pl.pallas_call(
        combine_kernel,
        grid=(steps,),
        in_specs=[
            pl.BlockSpec(s.shape, const),
            pl.BlockSpec(ids.shape, const),
            pl.BlockSpec(ids.shape, const),
            pl.BlockSpec((slots, cols), lambda j: (0, j)),
            pl.BlockSpec((slots, LANES), lambda j: (0, width // LANES)),
        ],
        out_specs=[pl.BlockSpec((tok_dev, cols), lambda j: (0, j)), pl.BlockSpec(ids.shape, const)],
        out_shape=[
            jax.ShapeDtypeStruct((tok_dev, width), BF),
            jax.ShapeDtypeStruct(ids.shape, F32),
        ],
        scratch_shapes=[pltpu.VMEM((tok_dev, slots), BF)],
        compiler_params=params(SMALL),
        cost_estimate=cost(2 * slots * tok_dev * width, 2 * (slots + tok_dev) * width),
        name="combine",
    )(s, ids, probs, back, back)


def exchange(rows):
    return lax.all_to_all(rows, "expert", split_axis=0, concat_axis=0, tiled=True)


def exchange(rows):
    return lax.all_to_all(rows, "expert", split_axis=0, concat_axis=0, tiled=True)


def on_device(tokens, grad_out, expert_ids, gate_probs, w_gate, w_up, w_down):
    groups = lax.axis_size("expert")
    ids, probs = expert_ids.T, gate_probs.T
    send, sel = route(ids, probs, tokens, grad_out, groups)
    recv = exchange(send)
    p = lax.axis_index("dp")
    x, core = p // 2, p % 2
    place = jnp.stack([core, (x + 2) % 4, (x + 1) % 4, (x + 3) % 4, x])
    dx, *pieces = rows_pass(place, recv, w_gate[0], w_up[0], w_down[0])
    slots = dx.shape[0]
    back = exchange(dx.reshape(groups, CAP, -1)).reshape(slots, -1)
    grads = finish(*reduce_parts(*pieces))
    sel, *grads = lax.optimization_barrier((sel, *grads))
    input_grad, gate_grad = combine(sel, ids, probs, back)
    return input_grad, gate_grad.T, *grads


def solution(mesh):
    row = P(("dp", "expert"), None)
    per_expert = P("expert", None, None)
    return jax.shard_map(
        on_device,
        mesh=mesh,
        in_specs=(row, row, row, row, per_expert, per_expert, per_expert),
        out_specs=(row, row, P("expert", "dp", None), P("expert", "dp", None), P("expert", None, "dp")),
        check_vma=False,
    )
```

```python
import functools
import jax
import jax.numpy as jnp
from jax import lax
from jax.experimental import pallas as pl
from jax.experimental.pallas import tpu as pltpu
from jax.sharding import PartitionSpec as P

CAP = 16
LANES = 128
BF = jnp.bfloat16
F32 = jnp.float32
VMEM_LIMIT = 56 * 1024 * 1024
SMALL = 16 * 1024 * 1024


def mm(a, b):
    return jnp.dot(a, b, preferred_element_type=F32)


def mm_nt(a, b):
    return lax.dot_general(a, b, (((1,), (1,)), ((), ())), preferred_element_type=F32)


def params(vmem=VMEM_LIMIT):
    return pltpu.CompilerParams(vmem_limit_bytes=vmem)


def cost(flops, nbytes):
    return pl.CostEstimate(flops=flops, bytes_accessed=nbytes, transcendentals=0)


def route_kernel(groups, ids_ref, probs_ref, tok_ref, dy_ref, out_ref, s_ref, sg_ref):
    topk, tok_dev = ids_ref.shape

    @pl.when(pl.program_id(0) == 0)
    def _():
        ids = ids_ref[...]
        probs = probs_ref[...].astype(F32)
        expert = lax.broadcasted_iota(jnp.int32, (groups, tok_dev), 0)
        hits = jnp.zeros((groups, tok_dev), F32)
        gate = jnp.zeros((groups, tok_dev), F32)
        for k in range(topk):
            hit = ids[k : k + 1] == expert
            hits = jnp.where(hit, 1.0, hits)
            gate = jnp.where(hit, probs[k : k + 1], gate)
        row = lax.broadcasted_iota(jnp.int32, (tok_dev, tok_dev), 0)
        col = lax.broadcasted_iota(jnp.int32, (tok_dev, tok_dev), 1)
        before = jnp.where(row < col, 1.0, 0.0).astype(BF)
        rank = mm(hits.astype(BF), before)
        rank = jnp.where(hits > 0.0, rank, -1.0).astype(jnp.int32)
        slot = lax.broadcasted_iota(jnp.int32, (groups, CAP, tok_dev), 1)
        sel = rank[:, None, :] == slot
        s_ref[...] = jnp.where(sel, 1.0, 0.0).reshape(groups * CAP, tok_dev).astype(BF)
        sg_ref[...] = (
            jnp.where(sel, jnp.broadcast_to(gate[:, None, :], sel.shape), 0.0)
            .reshape(groups * CAP, tok_dev)
            .astype(BF)
        )

    cols = tok_ref.shape[1]
    x = mm(s_ref[...], tok_ref[...]).astype(BF)
    out_ref[:, :CAP, :] = x.reshape(groups, CAP, cols)
    gy = mm(sg_ref[...], dy_ref[...]).astype(BF)
    out_ref[:, CAP:, :] = gy.reshape(groups, CAP, cols)


def route(ids, probs, tokens, grad_out, groups):
    tok_dev, width = tokens.shape
    topk = ids.shape[0]
    slots = groups * CAP
    steps = 2
    cols = width // steps
    const = lambda j: (0, 0)
    return pl.pallas_call(
        functools.partial(route_kernel, groups),
        grid=(steps,),
        in_specs=[
            pl.BlockSpec((topk, tok_dev), const),
            pl.BlockSpec((topk, tok_dev), const),
            pl.BlockSpec((tok_dev, cols), lambda j: (0, j)),
            pl.BlockSpec((tok_dev, cols), lambda j: (0, j)),
        ],
        out_specs=[
            pl.BlockSpec((groups, 2 * CAP, cols), lambda j: (0, 0, j)),
            pl.BlockSpec((slots, tok_dev), const),
        ],
        out_shape=[
            jax.ShapeDtypeStruct((groups, 2 * CAP, width), BF),
            jax.ShapeDtypeStruct((slots, tok_dev), BF),
        ],
        scratch_shapes=[pltpu.VMEM((slots, tok_dev), BF)],
        compiler_params=params(),
        cost_estimate=cost(4 * slots * tok_dev * width, 4 * (slots + tok_dev) * width),
        name="route",
    )(ids, probs, tokens, grad_out)


def mm_tn(a, b):
    return lax.dot_general(a, b, (((0,), (0,)), ((), ())), preferred_element_type=F32)


def rows_kernel(
    place_ref, recv_hbm, wg_hbm, wu_hbm, wd_hbm, dx_hbm, own_hbm, send_hbm,
    x_s, gy_s, wg_s, wu_s, wd_s, dx_s, units_s, in_sems, out_sems, cols_sems,
):
    groups, _, width = recv_hbm.shape
    rows = groups * CAP
    loads = [
        pltpu.make_async_copy(recv_hbm.at[:, :CAP, :], x_s, in_sems.at[0]),
        pltpu.make_async_copy(wg_hbm, wg_s, in_sems.at[1]),
        pltpu.make_async_copy(wu_hbm, wu_s, in_sems.at[2]),
        pltpu.make_async_copy(recv_hbm.at[:, CAP:, :], gy_s, in_sems.at[3]),
        pltpu.make_async_copy(wd_hbm, wd_s, in_sems.at[4]),
    ]
    for c in loads:
        c.start()
    stores = []

    def store(src, dst, sem):
        c = pltpu.make_async_copy(src, dst, sem)
        c.start()
        stores.append(c)

    loads[0].wait()
    loads[1].wait()
    x = x_s[...].reshape(rows, width)
    a = mm(x, wg_s[...])
    loads[2].wait()
    u = mm(x, wu_s[...])
    s = jax.nn.sigmoid(a)
    act = a * s
    fa = u * (s * (1.0 + a * (1.0 - s)))
    units_s[0] = (act * u).astype(BF).reshape(units_s.shape[1:])
    loads[3].wait()
    loads[4].wait()
    core, part = place_ref[0], width // 8
    for i, dst in ((0, own_hbm), (1, send_hbm)):
        for k in range(9):
            which = 2 * place_ref[1 + k // 2 % 4] + (core if i == 0 else 1 - core)
            cols = pl.ds(pl.multiple_of(which * part, part), part)
            src = gy_s if k % 2 else x_s
            at = slice(k % 3 * part, (k % 3 + 1) * part)
            store(src.at[:, :, cols], dst.at[3 + k // 3, :, :, at], cols_sems.at[9 * i + k])
    dh = mm_nt(gy_s[...].reshape(rows, width), wd_s[...])
    units_s[1] = (dh * fa).astype(BF).reshape(units_s.shape[1:])
    units_s[2] = (dh * act).astype(BF).reshape(units_s.shape[1:])
    store(units_s, own_hbm.at[:3], out_sems.at[2])
    store(units_s, send_hbm.at[:3], out_sems.at[3])
    h, da, du = (units_s[i].reshape(rows, units_s.shape[3]) for i in range(3))
    r = jnp.sum(dh * h.astype(F32), axis=1, keepdims=True)
    dx_s[:, width:] = jnp.broadcast_to(r, (rows, LANES)).astype(BF)
    cut = width // 2
    for i, lo, hi, end in ((0, 0, cut, cut), (1, cut, width, width + LANES)):
        dx = mm_nt(da, wg_s[lo:hi, :]) + mm_nt(du, wu_s[lo:hi, :])
        dx_s[:, lo:hi] = dx.astype(BF)
        store(dx_s.at[:, lo:end], dx_hbm.at[:, lo:end], out_sems.at[i])
    for c in stores:
        c.wait()


def rows_pass(place, recv, wg, wu, wd):
    groups, _, width = recv.shape
    rows = groups * CAP
    hid = wg.shape[1]
    hbm = pl.BlockSpec(memory_space=pl.ANY)
    pack = jax.ShapeDtypeStruct((6, groups, CAP, hid), BF)
    return pl.pallas_call(
        rows_kernel,
        in_specs=[pl.BlockSpec(memory_space=pltpu.SMEM)] + [hbm] * 4,
        out_specs=[hbm] * 3,
        out_shape=[jax.ShapeDtypeStruct((rows, width + LANES), BF), pack, pack],
        scratch_shapes=[
            pltpu.VMEM((groups, CAP, width), BF),
            pltpu.VMEM((groups, CAP, width), BF),
            pltpu.VMEM(wg.shape, BF),
            pltpu.VMEM(wu.shape, BF),
            pltpu.VMEM(wd.shape, BF),
            pltpu.VMEM((rows, width + LANES), BF),
            pltpu.VMEM((3, groups, CAP, hid), BF),
            pltpu.SemaphoreType.DMA((5,)),
            pltpu.SemaphoreType.DMA((4,)),
            pltpu.SemaphoreType.DMA((18,)),
        ],
        compiler_params=params(50 * 1024 * 1024),
        cost_estimate=cost(10 * rows * width * hid, 2 * (3 * rows * width + 3 * width * hid)),
        name="rows_pass",
    )(place, recv, wg, wu, wd)


def grad(refs, chunk, w, lo, hi):
    k = 2 * chunk + (1 if w == 0 else 0)
    total = 0.0
    for ref in refs:
        _, groups, cap, hid = ref.shape
        part = hid // 3
        cols = ref[3 + k // 3, :, :, k % 3 * part : (k % 3 + 1) * part].reshape(groups * cap, part)
        total = total + mm_tn(cols, ref[w, :, :, lo:hi].reshape(groups * cap, hi - lo))
    return total


def first_kernel(*refs):
    refs, (far_a, far_b, near_b, near_a) = refs[:2], refs[2:]
    hid = refs[0].shape[3]
    half = hid // 2
    for w in range(3):
        t = grad(refs, 0, w, 0, hid).astype(BF)
        far_a[w] = t[:, :half]
        far_b[w] = t[:, half:]
        near_b[w] = grad(refs, 1, w, half, hid).astype(BF)
        near_a[w] = grad(refs, 2, w, 0, half).astype(BF)


def second_kernel(*refs):
    refs, (left, right, sum_left, sum_right) = refs[:2], refs[2:]
    hid = refs[0].shape[3]
    half = hid // 2
    for w in range(3):
        sum_left[w] = (grad(refs, 1, w, 0, half) + left[w].astype(F32)).astype(BF)
        sum_right[w] = (grad(refs, 2, w, half, hid) + right[w].astype(F32)).astype(BF)


def third_kernel(*refs):
    refs, (left, right, out) = refs[:2], refs[2:]
    hid = refs[0].shape[3]
    half = hid // 2
    for w in range(3):
        t = grad(refs, 3, w, 0, hid)
        out[0, w] = (t[:, :half] + right[w].astype(F32)).astype(BF)
        out[1, w] = (t[:, half:] + left[w].astype(F32)).astype(BF)


def part_call(kernel, name, outs, *args):
    return pl.pallas_call(
        kernel,
        out_shape=outs,
        compiler_params=params(20 * 1024 * 1024),
        name=name,
    )(*args)


def reduce_parts(own, send):
    swap = lambda t: lax.ppermute(t, "dp", [(i, i ^ 1) for i in range(8)])
    shift = lambda t, d: lax.ppermute(t, "dp", [(i, (i + 2 * d) % 8) for i in range(8)])
    rows = own, swap(send)
    hid = own.shape[3]
    part, half = hid // 3, hid // 2
    piece = jax.ShapeDtypeStruct((3, part, half), BF)
    far_a, far_b, near_b, near_a = part_call(first_kernel, "first_parts", [piece] * 4, *rows)
    from_left, from_right = shift(far_a, 1), shift(far_b, -1)
    plain_left, plain_right = shift(near_b, 1), shift(near_a, -1)
    sums = part_call(second_kernel, "second_parts", [piece] * 2, *rows, from_left, from_right)
    mine = jax.ShapeDtypeStruct((2, 3, part, half), BF)
    total = part_call(third_kernel, "third_parts", mine, *rows, plain_left, plain_right)
    return total, shift(sums[0], 1), shift(sums[1], -1)


def finish_kernel(sum_ref, left_ref, right_ref, g_ref, u_ref, d_ref):
    half = sum_ref.shape[3]
    for i, ref in ((0, left_ref), (1, right_ref)):
        t = (sum_ref[i].astype(F32) + ref[...].astype(F32)).astype(BF)
        cols = slice(i * half, (i + 1) * half)
        d_ref[0, cols, :] = t[0].T
        g_ref[0, :, cols] = t[1]
        u_ref[0, :, cols] = t[2]


def finish(total, left, right):
    _, _, part, half = total.shape
    hid = 2 * half
    return pl.pallas_call(
        finish_kernel,
        out_shape=[
            jax.ShapeDtypeStruct((1, part, hid), BF),
            jax.ShapeDtypeStruct((1, part, hid), BF),
            jax.ShapeDtypeStruct((1, hid, part), BF),
        ],
        compiler_params=params(SMALL),
        name="finish",
    )(total, left, right)


def combine_kernel(s_ref, ids_ref, probs_ref, back_ref, r_ref, dx_ref, gg_ref, st_ref):
    groups = s_ref.shape[0] // CAP
    topk, tok_dev = ids_ref.shape

    @pl.when(pl.program_id(0) == 0)
    def _():
        s = s_ref[...]
        st_ref[...] = s.T
        r = r_ref[...].astype(F32) * s.astype(F32)
        r = jnp.sum(r.reshape(groups, CAP, tok_dev), axis=1)
        ids = ids_ref[...]
        expert = lax.broadcasted_iota(jnp.int32, (groups, tok_dev), 0)
        for k in range(topk):
            v = jnp.sum(jnp.where(expert == ids[k : k + 1], r, 0.0), axis=0, keepdims=True)
            gg_ref[k : k + 1] = v / probs_ref[k : k + 1].astype(F32)

    dx_ref[...] = mm(st_ref[...], back_ref[...]).astype(BF)


def combine(s, ids, probs, back):
    slots, tok_dev = s.shape
    width = back.shape[1] - LANES
    steps = 1
    cols = width // steps
    const = lambda j: (0, 0)
    return pl.pallas_call(
        combine_kernel,
        grid=(steps,),
        in_specs=[
            pl.BlockSpec(s.shape, const),
            pl.BlockSpec(ids.shape, const),
            pl.BlockSpec(ids.shape, const),
            pl.BlockSpec((slots, cols), lambda j: (0, j)),
            pl.BlockSpec((slots, LANES), lambda j: (0, width // LANES)),
        ],
        out_specs=[pl.BlockSpec((tok_dev, cols), lambda j: (0, j)), pl.BlockSpec(ids.shape, const)],
        out_shape=[
            jax.ShapeDtypeStruct((tok_dev, width), BF),
            jax.ShapeDtypeStruct(ids.shape, F32),
        ],
        scratch_shapes=[pltpu.VMEM((tok_dev, slots), BF)],
        compiler_params=params(SMALL),
        cost_estimate=cost(2 * slots * tok_dev * width, 2 * (slots + tok_dev) * width),
        name="combine",
    )(s, ids, probs, back, back)


def exchange(rows):
    return lax.all_to_all(rows, "expert", split_axis=0, concat_axis=0, tiled=True)


def exchange(rows):
    return lax.all_to_all(rows, "expert", split_axis=0, concat_axis=0, tiled=True)


def on_device(tokens, grad_out, expert_ids, gate_probs, w_gate, w_up, w_down):
    groups = lax.axis_size("expert")
    ids, probs = expert_ids.T, gate_probs.T
    send, sel = route(ids, probs, tokens, grad_out, groups)
    recv = exchange(send)
    p = lax.axis_index("dp")
    x, core = p // 2, p % 2
    place = jnp.stack([core, (x + 2) % 4, (x + 1) % 4, (x + 3) % 4, x])
    dx, *pieces = rows_pass(place, recv, w_gate[0], w_up[0], w_down[0])
    slots = dx.shape[0]
    back = exchange(dx.reshape(groups, CAP, -1)).reshape(slots, -1)
    grads = finish(*reduce_parts(*pieces))
    sel, *grads = lax.optimization_barrier((sel, *grads))
    input_grad, gate_grad = combine(sel, ids, probs, back)
    return input_grad, gate_grad.T, *grads


def solution(mesh):
    row = P(("dp", "expert"), None)
    per_expert = P("expert", None, None)
    return jax.shard_map(
        on_device,
        mesh=mesh,
        in_specs=(row, row, row, row, per_expert, per_expert, per_expert),
        out_specs=(row, row, P("expert", "dp", None), P("expert", "dp", None), P("expert", None, "dp")),
        check_vma=False,
    )
```
